32 devices in a mesh: seq: 4 (over y, x), tensor: 8 (over z, core).
Axes of the slice: x: 2, y: 2, z: 4, core: 2. Of those that a mesh axis runs over, the one named last changes fastest.
Arguments:
- hidden_in: bfloat16 [4096, 2304], P(('seq', 'tensor')), may hold values from -6 to 6
- norm_attn: float32 [2304], replicated, may hold values from 0.1 to 1.9
- norm_ffn: float32 [2304], replicated, may hold values from 0.1 to 1.9
- w_qkv: bfloat16 [3, 2304, 512], P(None, None, 'tensor'), may hold values from -1 to 1
- w_out: bfloat16 [512, 2304], P('tensor'), may hold values from -0.25 to 0.25
- w_router: float32 [2304, 8], replicated, may hold values from -4 to 4
- w_gate_up: bfloat16 [2, 23040, 2304], P(None, 'tensor'), may hold values from -0.125 to 0.125
- w_down: bfloat16 [23040, 2304], P('tensor'), may hold values from -0.109375 to 0.109375
- segment_ids: int32 [4096], P('seq'), may hold values from 0 to 7, never falling along the last dimension, each value on 1 to 3072 neighbouring positions
- expert_ids: int32 [4096, 2], P(('seq', 'tensor')), may hold values from 0 to 7, all different within a row; in each aligned block of 128 rows (0 to 127, 128 to 255, ...) at most 64 rows name the same one
Outputs:
- hidden_out: bfloat16 [4096, 2304], P(('seq', 'tensor'))
- kv_cache: bfloat16 [8, 4096, 128], P('tensor', 'seq')
The draws below stay inside these ranges and needn't reach their ends.
Inputs may be any that keep to these rules, and one draw needn't show every extreme that they name: `segment_ids`: nondecreasing along the stream; each prompt has 1 to 3072 tokens and one has exactly 3072. `expert_ids`: the two experts of a token differ. Within each aligned block of 128 tokens (the tokens of one device), no expert is named by more than 64 tokens, a bound that some block reaches.
All inputs are finite; a program needn't handle non-finite values.
Results may differ from the reference program's by a relative error of at most 0.019.
Values may be sent and summed in bfloat16 or wider, within the bound.
A program may use at most 128 MiB of HBM per device.

```python
import math
import jax
import jax.numpy as jnp
import numpy as np
from jax import lax

D = 2304
HD = 64
EXPERTS = 8
FF = 2880
HEADS = 8
TOKENS = 4096
ROWS = 128
MOST = 64
SEGS = 8
SEG_MOST = 3072
N_TENSOR = 8


def draw_w_qkv(key, part):
    key_query = jax.random.fold_in(key, 0)
    key_noise = jax.random.fold_in(key, 2)
    key_value = jax.random.fold_in(key, 3)
    columns = HEADS * HD
    unit = D ** (-0.5)
    query_part = jnp.clip(jax.random.normal(key_query, (D, columns), jnp.float32) * unit, -1.0, 1.0)
    key_part = jnp.clip(jax.random.normal(key_noise, (D, columns), jnp.float32) * unit, -1.0, 1.0)
    value_part = jnp.clip(jax.random.normal(key_value, (D, columns), jnp.float32) * unit, -1.0, 1.0)
    return jnp.stack([query_part, key_part, value_part]).astype(jnp.bfloat16)


def draw_w_router(key, part):
    key_main = jax.random.fold_in(key, 0)
    values_drawn = jnp.clip(jax.random.normal(key_main, (D, EXPERTS), jnp.float32), -6.0, 6.0) * (2.0 * D ** (-0.5))
    return jnp.clip(values_drawn, -4.0, 4.0)


def steps_of(rng, extent, shards, low, largest):
    loudness = 1.0
    for position, blocks in shards:
        heights = jax.random.uniform(jax.random.fold_in(jax.random.fold_in(rng, 6), position), (blocks,), jnp.float32, low / len(shards), largest / len(shards))
        loudness = loudness * jnp.repeat(jnp.exp(heights), extent[position] // blocks).reshape((-1,) + (1,) * (len(extent) - 1 - position))
    return loudness


def split_up(count, total, limit, lean):
    portions = [(1 << 20) // math.isqrt(grade ** lean) + 1 for grade in range(2, count + 1)]
    surplus, given = total - limit - (count - 1), [1] * (count - 1)
    while surplus > 0:
        free = [i for i in range(count - 1) if given[i] < limit]
        mass, remaining = sum([portions[i] for i in free]), surplus
        for i in free:
            addition = min(limit - given[i], max(1, remaining * portions[i] // mass), surplus)
            given[i] = given[i] + addition
            surplus = surplus - addition
    return np.array([limit] + given)


def uneven(key, number_of, total, bound, lean):
    if number_of == 2:
        one = jax.random.randint(key, (), max(1, total - bound), min(bound, total - 1) + 1)
        return jnp.stack([one, total - one])
    lengths = jnp.asarray(split_up(number_of, total, bound, lean), jnp.int32)
    pairs = (number_of - 1) // 2
    source_of, sink = lengths[1:1 + 2 * pairs:2], lengths[2:2 + 2 * pairs:2]
    room = jnp.minimum(source_of - 1, bound - sink)
    moved = jax.random.randint(jax.random.fold_in(key, 1), (pairs,), 0, 1 << 20) % (room + 1)
    lengths = lengths.at[1:1 + 2 * pairs:2].set(source_of - moved).at[2:2 + 2 * pairs:2].set(sink + moved)
    return lengths[jax.random.permutation(jax.random.fold_in(key, 2), number_of)]


def shared_out(key, own, number, rows, count, top, most, skew):
    order = jax.random.permutation(key, count)
    crowded, common = load_shares(count, rows * top, most, skew, True), load_shares(count, rows * top, most, skew, False)
    places = jnp.arange(count)

    def named(tallies, offset_by):
        used = int((tallies > 0).sum())
        fixed = max(1, used // 4)
        passed = fixed + (places - fixed + offset_by * (used - fixed)) % max(1, count - fixed)
        return jnp.zeros((count,), jnp.int32).at[order[jnp.where(places < fixed, places, passed)]].set(jnp.asarray(tallies, jnp.int32))

    tallies = jnp.where(number % 4 == 0, named(crowded, number // 4), named(common, number - number // 4 - 1))
    mixed = jax.random.permutation(jax.random.fold_in(own, 3), count)
    source_of, sink = mixed[0:count // 2 * 2:2], mixed[1:count // 2 * 2:2]
    margin = jnp.minimum(tallies[source_of] - 1, most - tallies[sink]) // 2
    margin = jnp.where((source_of == order[0]) | (sink == order[0]) | (tallies[sink] == 0), 0, jnp.maximum(margin, 0))
    passed = jax.random.randint(jax.random.fold_in(own, 4), (count // 2,), 0, 1 << 20) % (margin + 1)
    tallies = tallies.at[source_of].add(-passed).at[sink].add(passed)
    labels = jnp.searchsorted(jnp.cumsum(tallies), jnp.arange(rows * top), side="right").astype(jnp.int32)
    listing = labels.reshape(top, rows).T
    listing = listing[jax.random.permutation(jax.random.fold_in(own, 1), rows)]
    offset_by = jax.random.randint(jax.random.fold_in(own, 2), (rows, 1), 0, top)
    return jnp.take_along_axis(listing, (jnp.arange(top)[None, :] + offset_by) % top, axis=1)


def load_shares(amount, total, reach, skew, full):
    weights = [(1 << 20) // math.isqrt(standing ** skew) + 1 for standing in range(1, amount + 1)]
    largest = reach if full else min(reach, max(-(-total // amount), total * weights[0] // sum(weights)))
    least = 1 if total - largest >= amount - 1 else 0
    given, spare = [largest] + [least] * (amount - 1), total - largest - least * (amount - 1)
    while spare > 0:
        free = [i for i in range(1, amount) if given[i] < largest] or [i for i in range(1, amount) if given[i] < reach]
        whole, left = sum([weights[i] for i in free]), spare
        for i in free:
            more = min(reach - given[i], max(1, left * weights[i] // whole), spare)
            given[i] = given[i] + more
            spare = spare - more
    return np.array(given)


def normal_values(rng, shape, spread, most, shards=(), kind=jnp.bfloat16):
    loudness = steps_of(rng, shape, shards, -0.22, 0.18) if shards else 1.0
    values = jax.random.normal(rng, shape, jnp.float32) * spread * loudness
    return jnp.minimum(jnp.maximum(values, -most), most).astype(kind)


def setup_inputs(seed: int = 0) -> dict:
    splits = jax.random.split(jax.random.key(seed), 11)
    hidden_in = normal_values(splits[0], (TOKENS, D), 1.0, 6.0, ((0, 32),))
    norm_attn = jnp.clip(1.0 + 0.18 * jax.random.normal(splits[1], (D,), jnp.float32), 0.1, 1.9)
    norm_ffn = jnp.clip(1.0 + 0.18 * jax.random.normal(splits[2], (D,), jnp.float32), 0.1, 1.9)
    w_qkv = draw_w_qkv(jax.random.fold_in(splits[10], 71), 0)
    w_out = normal_values(splits[4], (HEADS * HD, D), (HEADS * HD) ** -0.5, 0.25, ((0, 8),))
    w_router = draw_w_router(jax.random.fold_in(splits[10], 71), 0)
    w_gate_up = normal_values(splits[6], (2, EXPERTS * FF, D), D ** -0.5, 0.125, ((1, 8),))
    w_down = normal_values(splits[7], (EXPERTS * FF, D), FF ** -0.5, 0.109375, ((0, 8),))
    segment_ids = jnp.searchsorted(jnp.cumsum(uneven(splits[8], SEGS, TOKENS, SEG_MOST, 2)), jnp.arange(TOKENS), side="right").astype(jnp.int32)
    expert_ids_keys = jax.random.split(jax.random.fold_in(splits[9], 1), TOKENS // ROWS)
    expert_ids_turns = jax.random.permutation(jax.random.fold_in(splits[9], 3), TOKENS // ROWS)
    expert_ids = jax.vmap(lambda own, number: shared_out(jax.random.fold_in(splits[9], 2), own, number, ROWS, EXPERTS, 2, MOST, 2))(expert_ids_keys, expert_ids_turns).reshape((TOKENS, 2))
    return dict(hidden_in=hidden_in, norm_attn=norm_attn, norm_ffn=norm_ffn, w_qkv=w_qkv, w_out=w_out, w_router=w_router, w_gate_up=w_gate_up, w_down=w_down, segment_ids=segment_ids, expert_ids=expert_ids)


epsilon = 1e-06

def rms_norm(hidden_rows, gain):
    as_float = hidden_rows.astype(jnp.float32)
    scale = lax.rsqrt(lax.optimization_barrier(jnp.mean(as_float * as_float, axis=-1, keepdims=True)) + epsilon)
    return (as_float * scale * gain).astype(jnp.bfloat16)

def rotate(head_rows, positions):
    half_size = head_rows.shape[-1] // 2
    frequency = jnp.exp(jnp.arange(half_size, dtype=jnp.float32) * (-math.log(10000.0) / half_size))
    angles = positions.astype(jnp.float32)[:, None] * frequency[None, :]
    cosine = jnp.cos(angles)[:, None, :]
    sine_part = jnp.sin(angles)[:, None, :]
    front_half = head_rows[..., :half_size]
    back_half = head_rows[..., half_size:]
    return jnp.concatenate([front_half * cosine - back_half * sine_part, back_half * cosine + front_half * sine_part], axis=-1)

def gate_weight(slot_rows, slot_ids, own_expert, w_router):
    logits = jnp.dot(slot_rows.astype(jnp.float32), w_router, precision=lax.Precision.HIGHEST)
    expert_count = w_router.shape[1]
    one_hot = (slot_ids[:, :, None] == jnp.arange(expert_count, dtype=jnp.int32)[None, None, :]).astype(jnp.float32)
    chosen = lax.optimization_barrier(jnp.sum(one_hot * logits[:, None, :], axis=-1))
    gate_probs = jax.nn.softmax(chosen, axis=-1)
    return lax.optimization_barrier(jnp.sum(jnp.where(slot_ids == own_expert, gate_probs, 0.0), axis=-1))

def attend_head(query_rows, key_rows, value_rows, segment_ids, positions):
    token_count = query_rows.shape[0]
    block_size = math.gcd(token_count, 1024)

    def attend_block(block_start):
        query_block = lax.dynamic_slice_in_dim(query_rows, block_start, block_size, 0)
        segment_block = lax.dynamic_slice_in_dim(segment_ids, block_start, block_size, 0)
        position_block = lax.dynamic_slice_in_dim(positions, block_start, block_size, 0)
        scores = jnp.dot(query_block, key_rows.T, preferred_element_type=jnp.float32) * 0.125
        allowed = (segment_block[:, None] == segment_ids[None, :]) & (positions[None, :] <= position_block[:, None])
        masked = jnp.where(allowed, scores, -jnp.inf)
        top_score = lax.optimization_barrier(jnp.max(masked, axis=1, keepdims=True))
        weights = jnp.where(allowed, jnp.exp(masked - top_score), 0.0)
        denominator = lax.optimization_barrier(jnp.sum(weights, axis=1, keepdims=True))
        mixed = jnp.dot(weights.astype(jnp.bfloat16), value_rows, preferred_element_type=jnp.float32) / denominator
        return mixed.astype(jnp.bfloat16)
    block_starts = jnp.arange(token_count // block_size, dtype=jnp.int32) * block_size
    return lax.map(attend_block, block_starts).reshape(token_count, -1)

def reference(hidden_in, norm_attn, norm_ffn, w_qkv, w_out, w_router, w_gate_up, w_down, segment_ids, expert_ids):
    token_count = hidden_in.shape[0]
    model_width = hidden_in.shape[1]
    normed = rms_norm(hidden_in, norm_attn)
    positions = jnp.arange(token_count, dtype=jnp.int32)
    projected = jnp.einsum('td,cdh->cth', normed.astype(jnp.float32), w_qkv.astype(jnp.float32), precision=lax.Precision.HIGHEST)
    query_all = rotate(projected[0].reshape(token_count, HEADS, HD), positions).astype(jnp.bfloat16)
    key_all = rotate(projected[1].reshape(token_count, HEADS, HD), positions).astype(jnp.bfloat16)
    value_all = projected[2].reshape(token_count, HEADS, HD).astype(jnp.bfloat16)
    kv_cache = jnp.concatenate([key_all, value_all], axis=-1).transpose(1, 0, 2)
    per_group = HEADS // N_TENSOR
    query_heads = query_all.transpose(1, 0, 2)
    key_heads = key_all.transpose(1, 0, 2)
    value_heads = value_all.transpose(1, 0, 2)

    def head_group(carry, group_index):
        head_start = group_index * per_group
        query_group = lax.dynamic_slice_in_dim(query_heads, head_start, per_group, 0)
        key_group = lax.dynamic_slice_in_dim(key_heads, head_start, per_group, 0)
        value_group = lax.dynamic_slice_in_dim(value_heads, head_start, per_group, 0)
        outputs = lax.map(lambda head_item: attend_head(head_item[0], head_item[1], head_item[2], segment_ids, positions), (query_group, key_group, value_group))
        attended = outputs.transpose(1, 0, 2).reshape(token_count, per_group * HD)
        out_rows = lax.dynamic_slice_in_dim(w_out, head_start * HD, per_group * HD, 0)
        head_part = jnp.dot(attended, out_rows, preferred_element_type=jnp.float32)
        rounded = lax.optimization_barrier(head_part.astype(jnp.bfloat16))
        return (carry + rounded.astype(jnp.float32), None)
    attention_sum, _ = lax.scan(head_group, jnp.zeros((token_count, model_width), jnp.float32), jnp.arange(N_TENSOR, dtype=jnp.int32))
    residual = hidden_in.astype(jnp.float32) + attention_sum
    normed_ffn = rms_norm(residual, norm_ffn)
    slice_size = FF * EXPERTS // N_TENSOR
    slice_count = FF // slice_size
    entry_count = 2 * token_count
    flat_experts = expert_ids.reshape(-1)
    flat_tokens = jnp.arange(entry_count, dtype=jnp.int32) // 2
    sorted_order = jnp.argsort(flat_experts, stable=True)
    sorted_tokens = flat_tokens[sorted_order]
    expert_counts = lax.optimization_barrier(jnp.sum((flat_experts[:, None] == jnp.arange(EXPERTS, dtype=jnp.int32)[None, :]).astype(jnp.int32), axis=0))
    padded = (expert_counts + 127) // 128 * 128
    padded_end = jnp.cumsum(padded)
    padded_start = padded_end - padded
    sorted_start = jnp.cumsum(expert_counts) - expert_counts
    block_total = entry_count // 128 + EXPERTS

    def expert_block(carry, block_index):
        block_base = block_index * 128
        own_expert = jnp.minimum(jnp.sum((padded_end <= block_base).astype(jnp.int32)), EXPERTS - 1)
        offset = block_base - padded_start[own_expert] + jnp.arange(128, dtype=jnp.int32)
        is_live = offset < expert_counts[own_expert]
        entry_index = jnp.clip(sorted_start[own_expert] + offset, 0, entry_count - 1)
        token_rows = sorted_tokens[entry_index]
        slot_rows = jnp.where(is_live[:, None], normed_ffn[token_rows], jnp.zeros((), jnp.bfloat16))
        slot_ids = expert_ids[token_rows]
        weight = gate_weight(slot_rows, slot_ids, own_expert, w_router)
        block_sum = jnp.zeros((128, model_width), jnp.float32)
        for slice_index in range(slice_count):
            row_start = (own_expert * FF + slice_index * slice_size).astype(jnp.int32)
            gate_rows = lax.dynamic_slice_in_dim(w_gate_up[0], row_start, slice_size, 0)
            up_rows = lax.dynamic_slice_in_dim(w_gate_up[1], row_start, slice_size, 0)
            down_rows = lax.dynamic_slice_in_dim(w_down, row_start, slice_size, 0)
            gate_act = jnp.dot(slot_rows, gate_rows.T, preferred_element_type=jnp.float32)
            up_act = jnp.dot(slot_rows, up_rows.T, preferred_element_type=jnp.float32)
            hidden_act = (jax.nn.silu(gate_act) * up_act).astype(jnp.bfloat16)
            output = jnp.dot(hidden_act, down_rows, preferred_element_type=jnp.float32)
            term = lax.optimization_barrier((output * weight[:, None]).astype(jnp.bfloat16))
            block_sum = block_sum + term.astype(jnp.float32)
        block_sum = jnp.where(is_live[:, None], block_sum, 0.0)
        return (carry.at[token_rows].add(block_sum), None)
    expert_sum, _ = lax.scan(expert_block, jnp.zeros((token_count, model_width), jnp.float32), jnp.arange(block_total, dtype=jnp.int32))
    hidden_out = (residual + expert_sum).astype(jnp.bfloat16)
    return (hidden_out, kv_cache)
```

```python
import math

import jax
import jax.numpy as jnp
from jax import lax
from jax.sharding import PartitionSpec as P

HD = 64


epsilon = 1e-06
low_score = -1e30


def rms_norm(hidden_rows, gain):
    as_float = hidden_rows.astype(jnp.float32)
    scale = lax.rsqrt(jnp.mean(as_float * as_float, axis=-1, keepdims=True) + epsilon)
    return (as_float * scale * gain).astype(jnp.bfloat16)


def rotate(head_rows, positions):
    half_size = head_rows.shape[-1] // 2
    frequency = jnp.exp(jnp.arange(half_size, dtype=jnp.float32) * (-math.log(10000.0) / half_size))
    angles = positions.astype(jnp.float32)[:, None] * frequency[None, :]
    cosine = jnp.cos(angles)[:, None, :]
    sine_part = jnp.sin(angles)[:, None, :]
    front_half = head_rows[..., :half_size]
    back_half = head_rows[..., half_size:]
    return jnp.concatenate(
        [front_half * cosine - back_half * sine_part, back_half * cosine + front_half * sine_part],
        axis=-1,
    )


def fold_keys(
    softmax_state, query_rows, query_segments, query_positions, kv_rows, key_segments, key_start
):
    running_max, denominator, weighted_sum = softmax_state
    row_count = kv_rows.shape[0]
    block_size = math.gcd(row_count, 2048)
    head_size = query_rows.shape[-1]
    for block_start in range(0, row_count, block_size):
        kv_block = kv_rows[block_start : block_start + block_size]
        key_block = kv_block[..., :head_size]
        value_block = kv_block[..., head_size:]
        segment_block = key_segments[block_start : block_start + block_size]
        position_block = key_start + block_start + jnp.arange(block_size, dtype=jnp.int32)
        scores = (
            jnp.einsum("qhd,khd->hqk", query_rows, key_block, preferred_element_type=jnp.float32)
            * 0.125
        )
        allowed = (query_segments[:, None] == segment_block[None, :]) & (
            position_block[None, :] <= query_positions[:, None]
        )
        masked = jnp.where(allowed[None], scores, low_score)
        new_max = jnp.maximum(running_max, jnp.max(masked, axis=-1))
        weights = jnp.where(allowed[None], jnp.exp(masked - new_max[..., None]), 0.0)
        factor = jnp.exp(running_max - new_max)
        denominator = denominator * factor + jnp.sum(weights, axis=-1)
        weighted_sum = weighted_sum * factor[..., None] + jnp.einsum(
            "hqk,khd->hqd",
            weights.astype(jnp.bfloat16),
            value_block,
            preferred_element_type=jnp.float32,
        )
        running_max = new_max
    return (running_max, denominator, weighted_sum)


def slot_table(token_ids, target, slot_count):
    is_routed = jnp.any(token_ids == target, axis=1).astype(jnp.int32)
    places = jnp.arange(is_routed.shape[0], dtype=jnp.int32)
    slot_rank = jnp.sum(jnp.where(places[None, :] <= places[:, None], is_routed[None, :], 0), axis=1) - 1
    chosen_slot = (is_routed[None, :] == 1) & (
        slot_rank[None, :] == jnp.arange(slot_count, dtype=jnp.int32)[:, None]
    )
    return chosen_slot.astype(jnp.bfloat16)


def expert_apply(slot_rows, slot_ids, own_expert, w_router, w_gate_up, w_down):
    logits = jnp.dot(slot_rows.astype(jnp.float32), w_router, precision=lax.Precision.HIGHEST)
    expert_count = w_router.shape[1]
    one_hot = (
        slot_ids[:, :, None] == jnp.arange(expert_count, dtype=jnp.int32)[None, None, :]
    ).astype(jnp.float32)
    chosen = jnp.sum(one_hot * logits[:, None, :], axis=-1)
    gate_probs = jax.nn.softmax(chosen, axis=-1)
    weight = jnp.sum(jnp.where(slot_ids == own_expert, gate_probs, 0.0), axis=-1)
    contract = (((1,), (1,)), ((), ()))
    gate_act = lax.dot_general(
        slot_rows, w_gate_up[0], contract, preferred_element_type=jnp.float32
    )
    up_act = lax.dot_general(slot_rows, w_gate_up[1], contract, preferred_element_type=jnp.float32)
    hidden_act = (jax.nn.silu(gate_act) * up_act).astype(jnp.bfloat16)
    output = jnp.dot(hidden_act, w_down, preferred_element_type=jnp.float32)
    return (output * weight[:, None]).astype(jnp.bfloat16)


def shards(
    hidden_in,
    norm_attn,
    norm_ffn,
    w_qkv,
    w_out,
    w_router,
    w_gate_up,
    w_down,
    segment_ids,
    expert_ids,
):
    local_rows = hidden_in.shape[0]
    model_width = hidden_in.shape[1]
    tensor_count = lax.axis_size("tensor")
    tensor_place = lax.axis_index("tensor")
    seq_place = lax.axis_index("seq")
    group_rows = local_rows * tensor_count
    head_count = w_qkv.shape[2] // HD
    normed = rms_norm(hidden_in, norm_attn)
    projected = jnp.einsum(
        "td,cdh->tch",
        lax.all_gather(normed, "tensor", axis=0, tiled=True),
        w_qkv,
        preferred_element_type=jnp.float32,
    )
    positions = seq_place * group_rows + jnp.arange(group_rows, dtype=jnp.int32)
    query_rows = rotate(projected[:, 0].reshape(group_rows, head_count, HD), positions).astype(
        jnp.bfloat16
    )
    key_rows = rotate(projected[:, 1].reshape(group_rows, head_count, HD), positions).astype(
        jnp.bfloat16
    )
    value_rows = projected[:, 2].reshape(group_rows, head_count, HD).astype(jnp.bfloat16)
    kv_rows = jnp.concatenate([key_rows, value_rows], axis=-1)
    kv_cache = kv_rows.transpose(1, 0, 2)
    start_state = (
        jnp.full((head_count, group_rows), low_score, jnp.float32),
        jnp.zeros((head_count, group_rows), jnp.float32),
        jnp.zeros((head_count, group_rows, HD), jnp.float32),
    )
    softmax_state = fold_keys(
        start_state,
        query_rows,
        segment_ids,
        positions,
        lax.all_gather(kv_rows, "seq", axis=0, tiled=True),
        lax.all_gather(segment_ids, "seq", axis=0, tiled=True),
        jnp.int32(0),
    )
    running_max, denominator, weighted_sum = softmax_state
    attended = (
        (weighted_sum / denominator[..., None])
        .transpose(1, 0, 2)
        .reshape(group_rows, head_count * HD)
        .astype(jnp.bfloat16)
    )
    attention_sum = lax.psum_scatter(
        jnp.dot(attended, w_out, preferred_element_type=jnp.float32).astype(jnp.bfloat16),
        "tensor",
        scatter_dimension=0,
        tiled=True,
    ).astype(jnp.float32)
    residual = hidden_in.astype(jnp.float32) + attention_sum
    normed_ffn = rms_norm(residual, norm_ffn)
    expert_count = w_router.shape[1]
    slice_count = tensor_count // expert_count
    own_expert = tensor_place // slice_count
    slot_count = local_rows // 2
    full_rows, full_ids = (
        lax.all_gather(normed_ffn, "tensor", axis=0, tiled=True),
        lax.all_gather(expert_ids, "tensor", axis=0, tiled=True),
    )
    block_ids = full_ids.reshape(tensor_count, local_rows, 2)
    slot_tables = jax.vmap(lambda source_ids: slot_table(source_ids, own_expert, slot_count))(
        block_ids
    )
    slot_rows = jnp.einsum(
        "sjr,srd->sjd",
        slot_tables,
        full_rows.reshape(tensor_count, local_rows, model_width),
        preferred_element_type=jnp.float32,
    ).astype(jnp.bfloat16)
    slot_ids = jnp.einsum(
        "sjr,srk->sjk", slot_tables.astype(jnp.float32), block_ids.astype(jnp.float32)
    ).astype(jnp.int32)
    term_rows = expert_apply(
        slot_rows.reshape(-1, model_width),
        slot_ids.reshape(-1, 2),
        own_expert,
        w_router,
        w_gate_up,
        w_down,
    )
    placed = jnp.einsum(
        "sjr,sjd->srd",
        slot_tables,
        term_rows.reshape(tensor_count, slot_count, model_width),
        preferred_element_type=jnp.float32,
    ).reshape(group_rows, model_width)
    expert_sum = lax.psum_scatter(
        placed.astype(jnp.bfloat16), "tensor", scatter_dimension=0, tiled=True
    ).astype(jnp.float32)
    hidden_out = (residual + expert_sum).astype(jnp.bfloat16)
    return (hidden_out, kv_cache)


def solution(mesh):
    placed = (
        P(("seq", "tensor"), None),
        P(),
        P(),
        P(None, None, "tensor"),
        P("tensor", None),
        P(),
        P(None, "tensor", None),
        P("tensor", None),
        P("seq"),
        P(("seq", "tensor"), None),
    )
    return jax.shard_map(
        shards,
        mesh=mesh,
        in_specs=placed,
        out_specs=(P(("seq", "tensor"), None), P("tensor", "seq", None)),
        check_vma=False,
    )
```

```python
import math

import jax
import jax.numpy as jnp
from jax import lax
from jax.sharding import PartitionSpec as P

HD = 64


epsilon = 1e-06
low_score = -1e30


def rms_norm(hidden_rows, gain):
    as_float = hidden_rows.astype(jnp.float32)
    scale = lax.rsqrt(jnp.mean(as_float * as_float, axis=-1, keepdims=True) + epsilon)
    return (as_float * scale * gain).astype(jnp.bfloat16)


def rotate(head_rows, positions):
    half_size = head_rows.shape[-1] // 2
    frequency = jnp.exp(jnp.arange(half_size, dtype=jnp.float32) * (-math.log(10000.0) / half_size))
    angles = positions.astype(jnp.float32)[:, None] * frequency[None, :]
    cosine = jnp.cos(angles)[:, None, :]
    sine_part = jnp.sin(angles)[:, None, :]
    front_half = head_rows[..., :half_size]
    back_half = head_rows[..., half_size:]
    return jnp.concatenate(
        [front_half * cosine - back_half * sine_part, back_half * cosine + front_half * sine_part],
        axis=-1,
    )


def fold_keys(
    softmax_state, query_rows, query_segments, query_positions, kv_rows, key_segments, key_start
):
    running_max, denominator, weighted_sum = softmax_state
    row_count = kv_rows.shape[0]
    block_size = math.gcd(row_count, 2048)
    head_size = query_rows.shape[-1]
    for block_start in range(0, row_count, block_size):
        kv_block = kv_rows[block_start : block_start + block_size]
        key_block = kv_block[..., :head_size]
        value_block = kv_block[..., head_size:]
        segment_block = key_segments[block_start : block_start + block_size]
        position_block = key_start + block_start + jnp.arange(block_size, dtype=jnp.int32)
        scores = (
            jnp.einsum("qhd,khd->hqk", query_rows, key_block, preferred_element_type=jnp.float32)
            * 0.125
        )
        allowed = (query_segments[:, None] == segment_block[None, :]) & (
            position_block[None, :] <= query_positions[:, None]
        )
        masked = jnp.where(allowed[None], scores, low_score)
        new_max = jnp.maximum(running_max, jnp.max(masked, axis=-1))
        weights = jnp.where(allowed[None], jnp.exp(masked - new_max[..., None]), 0.0)
        factor = jnp.exp(running_max - new_max)
        denominator = denominator * factor + jnp.sum(weights, axis=-1)
        weighted_sum = weighted_sum * factor[:, None, :] + jnp.einsum(
            "hqk,khd->hdq",
            weights.astype(jnp.bfloat16),
            value_block,
            preferred_element_type=jnp.float32,
        )
        running_max = new_max
    return (running_max, denominator, weighted_sum)


def pack_ids(ids, width):
    flat = ids.reshape(-1).astype(jnp.bfloat16)
    row_count = -(-flat.shape[0] // (16 * width)) * 16
    return jnp.pad(flat, (0, row_count * width - flat.shape[0])).reshape(row_count, width)


def unpack_ids(packed, count):
    return packed.reshape(packed.shape[0], -1)[:, :count].astype(jnp.int32)


def slot_table(token_ids, target, slot_count):
    is_routed = jnp.any(token_ids == target, axis=1).astype(jnp.int32)
    places = jnp.arange(is_routed.shape[0], dtype=jnp.int32)
    slot_rank = jnp.sum(jnp.where(places[None, :] <= places[:, None], is_routed[None, :], 0), axis=1) - 1
    chosen_slot = (is_routed[None, :] == 1) & (
        slot_rank[None, :] == jnp.arange(slot_count, dtype=jnp.int32)[:, None]
    )
    return chosen_slot.astype(jnp.bfloat16)


def expert_apply(slot_rows, slot_ids, own_expert, w_router, w_gate_up, w_down):
    logits = jnp.dot(slot_rows.astype(jnp.float32), w_router, precision=lax.Precision.HIGHEST)
    expert_count = w_router.shape[1]
    one_hot = (
        slot_ids[:, :, None] == jnp.arange(expert_count, dtype=jnp.int32)[None, None, :]
    ).astype(jnp.float32)
    chosen = jnp.sum(one_hot * logits[:, None, :], axis=-1)
    gate_probs = jax.nn.softmax(chosen, axis=-1)
    weight = jnp.sum(jnp.where(slot_ids == own_expert, gate_probs, 0.0), axis=-1)
    contract = (((1,), (1,)), ((), ()))
    gate_act = lax.dot_general(
        slot_rows, w_gate_up[0], contract, preferred_element_type=jnp.float32
    )
    up_act = lax.dot_general(slot_rows, w_gate_up[1], contract, preferred_element_type=jnp.float32)
    hidden_act = (jax.nn.silu(gate_act) * up_act).astype(jnp.bfloat16)
    output = jnp.dot(hidden_act, w_down, preferred_element_type=jnp.float32)
    return (output * weight[:, None]).astype(jnp.bfloat16)


def shards(
    hidden_in,
    norm_attn,
    norm_ffn,
    w_qkv,
    w_out,
    w_router,
    w_gate_up,
    w_down,
    segment_ids,
    expert_ids,
):
    local_rows = hidden_in.shape[0]
    model_width = hidden_in.shape[1]
    tensor_count = lax.axis_size("tensor")
    tensor_place = lax.axis_index("tensor")
    seq_place = lax.axis_index("seq")
    group_rows = local_rows * tensor_count
    head_count = w_qkv.shape[2] // HD
    full_hidden = lax.all_gather(hidden_in, "tensor", axis=0, tiled=True)
    projected = jnp.einsum(
        "td,cdh->tch",
        rms_norm(full_hidden, norm_attn),
        w_qkv,
        preferred_element_type=jnp.float32,
    )
    positions = seq_place * group_rows + jnp.arange(group_rows, dtype=jnp.int32)
    query_rows = rotate(projected[:, 0].reshape(group_rows, head_count, HD), positions).astype(
        jnp.bfloat16
    )
    key_rows = rotate(projected[:, 1].reshape(group_rows, head_count, HD), positions).astype(
        jnp.bfloat16
    )
    value_rows = projected[:, 2].reshape(group_rows, head_count, HD).astype(jnp.bfloat16)
    kv_rows = jnp.concatenate([key_rows, value_rows], axis=-1)
    kv_cache = kv_rows.transpose(1, 0, 2)
    seq_count = lax.axis_size("seq")
    kv_flat = kv_cache.reshape(head_count * group_rows, 2 * HD)
    kv_packed = jnp.concatenate([kv_flat, pack_ids(segment_ids, 2 * HD)], axis=0)
    out_packed = jnp.concatenate([w_out, pack_ids(expert_ids, model_width)], axis=0)
    kv_packed, out_packed = lax.optimization_barrier((kv_packed, out_packed))
    kv_gathered = lax.all_gather(kv_packed, "seq", axis=0)
    out_gathered = lax.all_gather(out_packed, "tensor", axis=0)
    all_segments = unpack_ids(kv_gathered[:, kv_flat.shape[0] :], group_rows).reshape(-1)
    all_kv = (
        kv_gathered[:, : kv_flat.shape[0]]
        .reshape(seq_count, head_count, group_rows, 2 * HD)
        .transpose(0, 2, 1, 3)
        .reshape(seq_count * group_rows, head_count, 2 * HD)
    )
    full_ids = unpack_ids(out_gathered[:, w_out.shape[0] :], 2 * local_rows)
    w_out_full = out_gathered[:, : w_out.shape[0]].reshape(-1, model_width)
    start_state = (
        jnp.full((head_count, group_rows), low_score, jnp.float32),
        jnp.zeros((head_count, group_rows), jnp.float32),
        jnp.zeros((head_count, HD, group_rows), jnp.float32),
    )
    softmax_state = fold_keys(
        start_state, query_rows, segment_ids, positions, all_kv, all_segments, jnp.int32(0)
    )
    running_max, denominator, weighted_sum = softmax_state
    attended = (
        (weighted_sum / denominator[:, None, :])
        .astype(jnp.bfloat16)
        .reshape(head_count * HD, group_rows)
    )
    attention_sum = lax.dot_general(
        lax.all_gather(attended, "tensor", axis=0, tiled=True),
        w_out_full,
        (((0,), (0,)), ((), ())),
        preferred_element_type=jnp.float32,
    )
    full_residual = full_hidden.astype(jnp.float32) + attention_sum
    full_rows = rms_norm(full_residual, norm_ffn)
    residual = lax.dynamic_slice_in_dim(full_residual, tensor_place * local_rows, local_rows, 0)
    expert_count = w_router.shape[1]
    slice_count = tensor_count // expert_count
    own_expert = tensor_place // slice_count
    slot_count = local_rows // 2
    block_ids = full_ids.reshape(tensor_count, local_rows, 2)
    slot_tables = jax.vmap(lambda source_ids: slot_table(source_ids, own_expert, slot_count))(
        block_ids
    )
    slot_rows = jnp.einsum(
        "sjr,srd->sjd",
        slot_tables,
        full_rows.reshape(tensor_count, local_rows, model_width),
        preferred_element_type=jnp.float32,
    ).astype(jnp.bfloat16)
    slot_ids = jnp.einsum(
        "sjr,srk->sjk", slot_tables.astype(jnp.float32), block_ids.astype(jnp.float32)
    ).astype(jnp.int32)
    term_rows = expert_apply(
        slot_rows.reshape(-1, model_width),
        slot_ids.reshape(-1, 2),
        own_expert,
        w_router,
        w_gate_up,
        w_down,
    )
    placed = jnp.einsum(
        "sjr,sjd->srd",
        slot_tables,
        term_rows.reshape(tensor_count, slot_count, model_width),
        preferred_element_type=jnp.float32,
    ).reshape(group_rows, model_width)
    expert_sum = lax.psum_scatter(
        placed.astype(jnp.bfloat16), "tensor", scatter_dimension=0, tiled=True
    ).astype(jnp.float32)
    hidden_out = (residual + expert_sum).astype(jnp.bfloat16)
    return (hidden_out, kv_cache)


def solution(mesh):
    placed = (
        P(("seq", "tensor"), None),
        P(),
        P(),
        P(None, None, "tensor"),
        P("tensor", None),
        P(),
        P(None, "tensor", None),
        P("tensor", None),
        P("seq"),
        P(("seq", "tensor"), None),
    )
    return jax.shard_map(
        shards,
        mesh=mesh,
        in_specs=placed,
        out_specs=(P(("seq", "tensor"), None), P("tensor", "seq", None)),
        check_vma=False,
    )
```

```python
import math

import jax
import jax.numpy as jnp
from jax import lax
from jax.sharding import PartitionSpec as P

HD = 64


epsilon = 1e-06
low_score = -1e30


def rms_norm(hidden_rows, gain):
    as_float = hidden_rows.astype(jnp.float32)
    scale = lax.rsqrt(jnp.mean(as_float * as_float, axis=-1, keepdims=True) + epsilon)
    return (as_float * scale * gain).astype(jnp.bfloat16)


def rotate(head_rows, positions):
    half_size = head_rows.shape[-1] // 2
    frequency = jnp.exp(jnp.arange(half_size, dtype=jnp.float32) * (-math.log(10000.0) / half_size))
    angles = positions.astype(jnp.float32)[:, None] * frequency[None, :]
    cosine = jnp.cos(angles)[:, None, :]
    sine_part = jnp.sin(angles)[:, None, :]
    front_half = head_rows[..., :half_size]
    back_half = head_rows[..., half_size:]
    return jnp.concatenate(
        [front_half * cosine - back_half * sine_part, back_half * cosine + front_half * sine_part],
        axis=-1,
    )


def fold_keys(
    softmax_state, query_rows, query_segments, query_positions, kv_rows, key_segments, key_start
):
    running_max, denominator, weighted_sum = softmax_state
    row_count = kv_rows.shape[0]
    block_size = math.gcd(row_count, 2048)
    head_size = query_rows.shape[-1]
    for block_start in range(0, row_count, block_size):
        kv_block = kv_rows[block_start : block_start + block_size]
        key_block = kv_block[..., :head_size]
        value_block = kv_block[..., head_size:]
        segment_block = key_segments[block_start : block_start + block_size]
        position_block = key_start + block_start + jnp.arange(block_size, dtype=jnp.int32)
        scores = (
            jnp.einsum("qhd,khd->hqk", query_rows, key_block, preferred_element_type=jnp.float32)
            * 0.125
        )
        allowed = (query_segments[:, None] == segment_block[None, :]) & (
            position_block[None, :] <= query_positions[:, None]
        )
        masked = jnp.where(allowed[None], scores, low_score)
        new_max = jnp.maximum(running_max, jnp.max(masked, axis=-1))
        weights = jnp.where(allowed[None], jnp.exp(masked - new_max[..., None]), 0.0)
        factor = jnp.exp(running_max - new_max)
        denominator = denominator * factor + jnp.sum(weights, axis=-1)
        weighted_sum = weighted_sum * factor[:, None, :] + jnp.einsum(
            "hqk,khd->hdq",
            weights.astype(jnp.bfloat16),
            value_block,
            preferred_element_type=jnp.float32,
        )
        running_max = new_max
    return (running_max, denominator, weighted_sum)


def pack_ids(ids, width):
    flat = ids.reshape(-1).astype(jnp.bfloat16)
    row_count = -(-flat.shape[0] // (16 * width)) * 16
    return jnp.pad(flat, (0, row_count * width - flat.shape[0])).reshape(row_count, width)


def unpack_ids(packed, count):
    return packed.reshape(packed.shape[0], -1)[:, :count].astype(jnp.int32)


def slot_table(token_ids, target, slot_count):
    is_routed = jnp.any(token_ids == target, axis=1).astype(jnp.int32)
    places = jnp.arange(is_routed.shape[0], dtype=jnp.int32)
    slot_rank = jnp.sum(jnp.where(places[None, :] <= places[:, None], is_routed[None, :], 0), axis=1) - 1
    chosen_slot = (is_routed[None, :] == 1) & (
        slot_rank[None, :] == jnp.arange(slot_count, dtype=jnp.int32)[:, None]
    )
    return chosen_slot.astype(jnp.bfloat16)


def expert_apply(slot_rows, slot_ids, own_expert, w_router, w_gate_up, w_down):
    logits = jnp.dot(slot_rows.astype(jnp.float32), w_router, precision=lax.Precision.HIGHEST)
    expert_count = w_router.shape[1]
    one_hot = (
        slot_ids[:, :, None] == jnp.arange(expert_count, dtype=jnp.int32)[None, None, :]
    ).astype(jnp.float32)
    chosen = jnp.sum(one_hot * logits[:, None, :], axis=-1)
    gate_probs = jax.nn.softmax(chosen, axis=-1)
    weight = jnp.sum(jnp.where(slot_ids == own_expert, gate_probs, 0.0), axis=-1)
    contract = (((1,), (1,)), ((), ()))
    gate_act = lax.dot_general(
        slot_rows, w_gate_up[0], contract, preferred_element_type=jnp.float32
    )
    up_act = lax.dot_general(slot_rows, w_gate_up[1], contract, preferred_element_type=jnp.float32)
    hidden_act = (jax.nn.silu(gate_act) * up_act).astype(jnp.bfloat16)
    output = jnp.dot(hidden_act, w_down, preferred_element_type=jnp.float32)
    return (output * weight[:, None]).astype(jnp.bfloat16)


def shards(
    hidden_in,
    norm_attn,
    norm_ffn,
    w_qkv,
    w_out,
    w_router,
    w_gate_up,
    w_down,
    segment_ids,
    expert_ids,
):
    local_rows = hidden_in.shape[0]
    model_width = hidden_in.shape[1]
    tensor_count = lax.axis_size("tensor")
    tensor_place = lax.axis_index("tensor")
    seq_place = lax.axis_index("seq")
    group_rows = local_rows * tensor_count
    head_count = w_qkv.shape[2] // HD
    full_hidden = lax.all_gather(hidden_in, "tensor", axis=0, tiled=True)
    projected = jnp.einsum(
        "td,cdh->tch",
        rms_norm(full_hidden, norm_attn),
        w_qkv,
        preferred_element_type=jnp.float32,
    )
    positions = seq_place * group_rows + jnp.arange(group_rows, dtype=jnp.int32)
    query_rows = rotate(projected[:, 0].reshape(group_rows, head_count, HD), positions).astype(
        jnp.bfloat16
    )
    key_rows = rotate(projected[:, 1].reshape(group_rows, head_count, HD), positions).astype(
        jnp.bfloat16
    )
    value_rows = projected[:, 2].reshape(group_rows, head_count, HD).astype(jnp.bfloat16)
    kv_rows = jnp.concatenate([key_rows, value_rows], axis=-1)
    kv_cache = kv_rows.transpose(1, 0, 2)
    seq_count = lax.axis_size("seq")
    kv_flat = kv_cache.reshape(head_count * group_rows, 2 * HD)
    kv_packed = jnp.concatenate([kv_flat, pack_ids(segment_ids, 2 * HD)], axis=0)
    out_packed = jnp.concatenate([w_out, pack_ids(expert_ids, model_width)], axis=0)
    kv_packed, out_packed = lax.optimization_barrier((kv_packed, out_packed))
    kv_gathered = lax.all_gather(kv_packed, "seq", axis=0)
    out_gathered = lax.all_gather(out_packed, "tensor", axis=0)
    all_segments = unpack_ids(kv_gathered[:, kv_flat.shape[0] :], group_rows).reshape(-1)
    all_kv = (
        kv_gathered[:, : kv_flat.shape[0]]
        .reshape(seq_count, head_count, group_rows, 2 * HD)
        .transpose(0, 2, 1, 3)
        .reshape(seq_count * group_rows, head_count, 2 * HD)
    )
    full_ids = unpack_ids(out_gathered[:, w_out.shape[0] :], 2 * local_rows)
    w_out_full = out_gathered[:, : w_out.shape[0]].reshape(-1, model_width)
    start_state = (
        jnp.full((head_count, group_rows), low_score, jnp.float32),
        jnp.zeros((head_count, group_rows), jnp.float32),
        jnp.zeros((head_count, HD, group_rows), jnp.float32),
    )
    softmax_state = fold_keys(
        start_state, query_rows, segment_ids, positions, all_kv, all_segments, jnp.int32(0)
    )
    running_max, denominator, weighted_sum = softmax_state
    attended = (
        (weighted_sum / denominator[:, None, :])
        .astype(jnp.bfloat16)
        .reshape(head_count * HD, group_rows)
    )
    attended, w_out_full = lax.optimization_barrier((attended, w_out_full))
    attention_sum = lax.dot_general(
        lax.all_gather(attended, "tensor", axis=0, tiled=True),
        w_out_full,
        (((0,), (0,)), ((), ())),
        preferred_element_type=jnp.float32,
    )
    full_residual = full_hidden.astype(jnp.float32) + attention_sum
    full_rows = rms_norm(full_residual, norm_ffn)
    residual = lax.dynamic_slice_in_dim(full_residual, tensor_place * local_rows, local_rows, 0)
    expert_count = w_router.shape[1]
    slice_count = tensor_count // expert_count
    own_expert = tensor_place // slice_count
    slot_count = local_rows // 2
    block_ids = full_ids.reshape(tensor_count, local_rows, 2)
    slot_tables = jax.vmap(lambda source_ids: slot_table(source_ids, own_expert, slot_count))(
        block_ids
    )
    slot_rows = jnp.einsum(
        "sjr,srd->sjd",
        slot_tables,
        full_rows.reshape(tensor_count, local_rows, model_width),
        preferred_element_type=jnp.float32,
    ).astype(jnp.bfloat16)
    slot_ids = jnp.einsum(
        "sjr,srk->sjk", slot_tables.astype(jnp.float32), block_ids.astype(jnp.float32)
    ).astype(jnp.int32)
    term_rows = expert_apply(
        slot_rows.reshape(-1, model_width),
        slot_ids.reshape(-1, 2),
        own_expert,
        w_router,
        w_gate_up,
        w_down,
    )
    placed = jnp.einsum(
        "sjr,sjd->srd",
        slot_tables,
        term_rows.reshape(tensor_count, slot_count, model_width),
        preferred_element_type=jnp.float32,
    ).reshape(group_rows, model_width)
    expert_sum = lax.psum_scatter(
        placed.astype(jnp.bfloat16), "tensor", scatter_dimension=0, tiled=True
    ).astype(jnp.float32)
    hidden_out = (residual + expert_sum).astype(jnp.bfloat16)
    return (hidden_out, kv_cache)


def solution(mesh):
    placed = (
        P(("seq", "tensor"), None),
        P(),
        P(),
        P(None, None, "tensor"),
        P("tensor", None),
        P(),
        P(None, "tensor", None),
        P("tensor", None),
        P("seq"),
        P(("seq", "tensor"), None),
    )
    return jax.shard_map(
        shards,
        mesh=mesh,
        in_specs=placed,
        out_specs=(P(("seq", "tensor"), None), P("tensor", "seq", None)),
        check_vma=False,
    )
```

```python
import math

import jax
import jax.numpy as jnp
from jax import lax
from jax.sharding import PartitionSpec as P

HD = 64


epsilon = 1e-06
low_score = -1e30


def rms_norm(hidden_rows, gain):
    as_float = hidden_rows.astype(jnp.float32)
    scale = lax.rsqrt(jnp.mean(as_float * as_float, axis=-1, keepdims=True) + epsilon)
    return (as_float * scale * gain).astype(jnp.bfloat16)


def rotate(head_rows, positions):
    half_size = head_rows.shape[-1] // 2
    frequency = jnp.exp(jnp.arange(half_size, dtype=jnp.float32) * (-math.log(10000.0) / half_size))
    angles = positions.astype(jnp.float32)[:, None] * frequency[None, :]
    cosine = jnp.cos(angles)[:, None, :]
    sine_part = jnp.sin(angles)[:, None, :]
    front_half = head_rows[..., :half_size]
    back_half = head_rows[..., half_size:]
    return jnp.concatenate(
        [front_half * cosine - back_half * sine_part, back_half * cosine + front_half * sine_part],
        axis=-1,
    )


def fold_keys(
    softmax_state, query_rows, query_segments, query_positions, kv_rows, key_segments, key_start
):
    running_max, denominator, weighted_sum = softmax_state
    row_count = kv_rows.shape[0]
    block_size = math.gcd(row_count, 2048)
    head_size = query_rows.shape[-1]
    for block_start in range(0, row_count, block_size):
        kv_block = kv_rows[block_start : block_start + block_size]
        key_block = kv_block[..., :head_size]
        value_block = kv_block[..., head_size:]
        segment_block = key_segments[block_start : block_start + block_size]
        position_block = key_start + block_start + jnp.arange(block_size, dtype=jnp.int32)
        scores = (
            jnp.einsum("qhd,khd->hqk", query_rows, key_block, preferred_element_type=jnp.float32)
            * 0.125
        )
        allowed = (query_segments[:, None] == segment_block[None, :]) & (
            position_block[None, :] <= query_positions[:, None]
        )
        masked = jnp.where(allowed[None], scores, low_score)
        new_max = jnp.maximum(running_max, jnp.max(masked, axis=-1))
        weights = jnp.where(allowed[None], jnp.exp(masked - new_max[..., None]), 0.0)
        factor = jnp.exp(running_max - new_max)
        denominator = denominator * factor + jnp.sum(weights, axis=-1)
        weighted_sum = weighted_sum * factor[:, None, :] + jnp.einsum(
            "hqk,khd->hdq",
            weights.astype(jnp.bfloat16),
            value_block,
            preferred_element_type=jnp.float32,
        )
        running_max = new_max
    return (running_max, denominator, weighted_sum)


def pack_ids(ids, width):
    flat = ids.reshape(-1).astype(jnp.bfloat16)
    row_count = -(-flat.shape[0] // (16 * width)) * 16
    return jnp.pad(flat, (0, row_count * width - flat.shape[0])).reshape(row_count, width)


def unpack_ids(packed, count):
    row_count = -(-count // packed.shape[-1])
    used = packed[..., :row_count, :]
    return used.reshape(packed.shape[:-2] + (-1,))[..., :count].astype(jnp.int32)


def slot_table(token_ids, target, slot_count):
    is_routed = jnp.any(token_ids == target, axis=1).astype(jnp.int32)
    places = jnp.arange(is_routed.shape[0], dtype=jnp.int32)
    slot_rank = jnp.sum(jnp.where(places[None, :] <= places[:, None], is_routed[None, :], 0), axis=1) - 1
    chosen_slot = (is_routed[None, :] == 1) & (
        slot_rank[None, :] == jnp.arange(slot_count, dtype=jnp.int32)[:, None]
    )
    return chosen_slot.astype(jnp.bfloat16)


def expert_apply(slot_rows, slot_ids, own_expert, w_router, w_gate_up, w_down):
    logits = jnp.dot(slot_rows.astype(jnp.float32), w_router, precision=lax.Precision.HIGHEST)
    expert_count = w_router.shape[1]
    one_hot = (
        slot_ids[:, :, None] == jnp.arange(expert_count, dtype=jnp.int32)[None, None, :]
    ).astype(jnp.float32)
    chosen = jnp.sum(one_hot * logits[:, None, :], axis=-1)
    gate_probs = jax.nn.softmax(chosen, axis=-1)
    weight = jnp.sum(jnp.where(slot_ids == own_expert, gate_probs, 0.0), axis=-1)
    contract = (((1,), (1,)), ((), ()))
    gate_act = lax.dot_general(
        slot_rows, w_gate_up[0], contract, preferred_element_type=jnp.float32
    )
    up_act = lax.dot_general(slot_rows, w_gate_up[1], contract, preferred_element_type=jnp.float32)
    hidden_act = (jax.nn.silu(gate_act) * up_act).astype(jnp.bfloat16)
    output = jnp.dot(hidden_act, w_down, preferred_element_type=jnp.float32)
    return (output * weight[:, None]).astype(jnp.bfloat16)


def shards(
    hidden_in,
    norm_attn,
    norm_ffn,
    w_qkv,
    w_out,
    w_router,
    w_gate_up,
    w_down,
    segment_ids,
    expert_ids,
):
    local_rows = hidden_in.shape[0]
    model_width = hidden_in.shape[1]
    tensor_count = lax.axis_size("tensor")
    tensor_place = lax.axis_index("tensor")
    seq_place = lax.axis_index("seq")
    group_rows = local_rows * tensor_count
    head_count = w_qkv.shape[2] // HD
    full_hidden = lax.all_gather(hidden_in, "tensor", axis=0, tiled=True)
    projected = jnp.einsum(
        "td,cdh->tch",
        rms_norm(full_hidden, norm_attn),
        w_qkv,
        preferred_element_type=jnp.float32,
    )
    positions = seq_place * group_rows + jnp.arange(group_rows, dtype=jnp.int32)
    query_rows = rotate(projected[:, 0].reshape(group_rows, head_count, HD), positions).astype(
        jnp.bfloat16
    )
    key_rows = rotate(projected[:, 1].reshape(group_rows, head_count, HD), positions).astype(
        jnp.bfloat16
    )
    value_rows = projected[:, 2].reshape(group_rows, head_count, HD).astype(jnp.bfloat16)
    kv_rows = jnp.concatenate([key_rows, value_rows], axis=-1)
    kv_cache = kv_rows.transpose(1, 0, 2)
    seq_count = lax.axis_size("seq")
    kv_flat = kv_cache.reshape(head_count * group_rows, 2 * HD)
    kv_packed = jnp.concatenate([kv_flat, pack_ids(segment_ids, 2 * HD)], axis=0)
    out_packed = jnp.concatenate([w_out, pack_ids(expert_ids, model_width)], axis=0)
    kv_packed, out_packed = lax.optimization_barrier((kv_packed, out_packed))
    arrivals = []
    for step in range(1, seq_count):
        pairs = [(i, i ^ step) for i in range(seq_count)]
        arrivals.append((lax.ppermute(kv_packed, "seq", pairs), seq_place ^ step))
    out_gathered = lax.all_gather(out_packed, "tensor", axis=0)
    full_ids = unpack_ids(out_gathered[:, w_out.shape[0] :], 2 * local_rows)
    w_out_full = out_gathered[:, : w_out.shape[0]].reshape(-1, model_width)
    start_state = (
        jnp.full((head_count, group_rows), low_score, jnp.float32),
        jnp.zeros((head_count, group_rows), jnp.float32),
        jnp.zeros((head_count, HD, group_rows), jnp.float32),
    )
    softmax_state = fold_keys(
        start_state,
        query_rows,
        segment_ids,
        positions,
        kv_rows,
        segment_ids,
        seq_place * group_rows,
    )
    for arrived, source in arrivals:
        softmax_state = fold_keys(
            softmax_state,
            query_rows,
            segment_ids,
            positions,
            arrived[: kv_flat.shape[0]]
            .reshape(head_count, group_rows, 2 * HD)
            .transpose(1, 0, 2),
            unpack_ids(arrived[kv_flat.shape[0] :], group_rows),
            source * group_rows,
        )
    running_max, denominator, weighted_sum = softmax_state
    attended = (
        (weighted_sum / denominator[:, None, :])
        .astype(jnp.bfloat16)
        .reshape(head_count * HD, group_rows)
    )
    attended, w_out_full = lax.optimization_barrier((attended, w_out_full))
    attention_sum = lax.dot_general(
        lax.all_gather(attended, "tensor", axis=0, tiled=True),
        w_out_full,
        (((0,), (0,)), ((), ())),
        preferred_element_type=jnp.float32,
    )
    full_residual = full_hidden.astype(jnp.float32) + attention_sum
    full_rows = rms_norm(full_residual, norm_ffn)
    residual = lax.dynamic_slice_in_dim(full_residual, tensor_place * local_rows, local_rows, 0)
    expert_count = w_router.shape[1]
    slice_count = tensor_count // expert_count
    own_expert = tensor_place // slice_count
    slot_count = local_rows // 2
    block_ids = full_ids.reshape(tensor_count, local_rows, 2)
    slot_tables = jax.vmap(lambda source_ids: slot_table(source_ids, own_expert, slot_count))(
        block_ids
    )
    slot_rows = jnp.einsum(
        "sjr,srd->sjd",
        slot_tables,
        full_rows.reshape(tensor_count, local_rows, model_width),
        preferred_element_type=jnp.float32,
    ).astype(jnp.bfloat16)
    slot_ids = jnp.einsum(
        "sjr,srk->sjk", slot_tables.astype(jnp.float32), block_ids.astype(jnp.float32)
    ).astype(jnp.int32)
    term_rows = expert_apply(
        slot_rows.reshape(-1, model_width),
        slot_ids.reshape(-1, 2),
        own_expert,
        w_router,
        w_gate_up,
        w_down,
    )
    placed = jnp.einsum(
        "sjr,sjd->srd",
        slot_tables,
        term_rows.reshape(tensor_count, slot_count, model_width),
        preferred_element_type=jnp.float32,
    ).reshape(group_rows, model_width)
    expert_sum = lax.psum_scatter(
        placed.astype(jnp.bfloat16), "tensor", scatter_dimension=0, tiled=True
    ).astype(jnp.float32)
    hidden_out = (residual + expert_sum).astype(jnp.bfloat16)
    return (hidden_out, kv_cache)


def solution(mesh):
    placed = (
        P(("seq", "tensor"), None),
        P(),
        P(),
        P(None, None, "tensor"),
        P("tensor", None),
        P(),
        P(None, "tensor", None),
        P("tensor", None),
        P("seq"),
        P(("seq", "tensor"), None),
    )
    return jax.shard_map(
        shards,
        mesh=mesh,
        in_specs=placed,
        out_specs=(P(("seq", "tensor"), None), P("tensor", "seq", None)),
        check_vma=False,
    )
```

```python
import functools
import math

import jax
import jax.numpy as jnp
from jax import lax
from jax.experimental import pallas as pl
from jax.experimental.pallas import tpu as pltpu
from jax.sharding import PartitionSpec as P

HD = 64


epsilon = 1e-06
low_score = -1e30


def rms_norm(hidden_rows, gain):
    as_float = hidden_rows.astype(jnp.float32)
    scale = lax.rsqrt(jnp.mean(as_float * as_float, axis=-1, keepdims=True) + epsilon)
    return (as_float * scale * gain).astype(jnp.bfloat16)


def rotate(head_rows, positions):
    half_size = head_rows.shape[-1] // 2
    frequency = jnp.exp(jnp.arange(half_size, dtype=jnp.float32) * (-math.log(10000.0) / half_size))
    angles = positions.astype(jnp.float32)[:, None] * frequency[None, :]
    cosine = jnp.cos(angles)[:, None, :]
    sine_part = jnp.sin(angles)[:, None, :]
    front_half = head_rows[..., :half_size]
    back_half = head_rows[..., half_size:]
    return jnp.concatenate(
        [front_half * cosine - back_half * sine_part, back_half * cosine + front_half * sine_part],
        axis=-1,
    )


def fold_keys(
    softmax_state, query_rows, query_segments, query_positions, kv_rows, key_segments, key_start
):
    running_max, denominator, weighted_sum = softmax_state
    row_count = kv_rows.shape[0]
    block_size = math.gcd(row_count, 2048)
    head_size = query_rows.shape[-1]
    for block_start in range(0, row_count, block_size):
        kv_block = kv_rows[block_start : block_start + block_size]
        key_block = kv_block[..., :head_size]
        value_block = kv_block[..., head_size:]
        segment_block = key_segments[block_start : block_start + block_size]
        position_block = key_start + block_start + jnp.arange(block_size, dtype=jnp.int32)
        scores = (
            jnp.einsum("qhd,khd->hqk", query_rows, key_block, preferred_element_type=jnp.float32)
            * 0.125
        )
        allowed = (query_segments[:, None] == segment_block[None, :]) & (
            position_block[None, :] <= query_positions[:, None]
        )
        masked = jnp.where(allowed[None], scores, low_score)
        new_max = jnp.maximum(running_max, jnp.max(masked, axis=-1))
        weights = jnp.where(allowed[None], jnp.exp(masked - new_max[..., None]), 0.0)
        factor = jnp.exp(running_max - new_max)
        denominator = denominator * factor + jnp.sum(weights, axis=-1)
        weighted_sum = weighted_sum * factor[:, None, :] + jnp.einsum(
            "hqk,khd->hdq",
            weights.astype(jnp.bfloat16),
            value_block,
            preferred_element_type=jnp.float32,
        )
        running_max = new_max
    return (running_max, denominator, weighted_sum)


def pack_ids(ids, width):
    flat = ids.reshape(-1).astype(jnp.bfloat16)
    row_count = -(-flat.shape[0] // (16 * width)) * 16
    return jnp.pad(flat, (0, row_count * width - flat.shape[0])).reshape(row_count, width)


def unpack_ids(packed, count):
    row_count = -(-count // packed.shape[-1])
    used = packed[..., :row_count, :]
    return used.reshape(packed.shape[:-2] + (-1,))[..., :count].astype(jnp.int32)


def slot_table(token_ids, target, slot_count):
    is_routed = jnp.any(token_ids == target, axis=1).astype(jnp.int32)
    places = jnp.arange(is_routed.shape[0], dtype=jnp.int32)
    slot_rank = jnp.sum(jnp.where(places[None, :] <= places[:, None], is_routed[None, :], 0), axis=1) - 1
    chosen_slot = (is_routed[None, :] == 1) & (
        slot_rank[None, :] == jnp.arange(slot_count, dtype=jnp.int32)[:, None]
    )
    return chosen_slot.astype(jnp.bfloat16)


def ffn_kernel(step_count, rows_ref, weight_ref, gate_up_ref, down_ref, out_ref, total_ref):
    step = pl.program_id(0)
    contract = (((1,), (1,)), ((), ()))
    rows = rows_ref[...]
    gate_act = lax.dot_general(rows, gate_up_ref[0], contract, preferred_element_type=jnp.float32)
    up_act = lax.dot_general(rows, gate_up_ref[1], contract, preferred_element_type=jnp.float32)
    hidden_act = (gate_act / (1.0 + jnp.exp(-gate_act)) * up_act).astype(jnp.bfloat16)

    @pl.when(step == 0)
    def _():
        total_ref[...] = jnp.zeros_like(total_ref)

    total_ref[...] += jnp.dot(hidden_act, down_ref[...], preferred_element_type=jnp.float32)

    @pl.when(step == step_count - 1)
    def _():
        out_ref[...] = (total_ref[...] * weight_ref[...]).astype(out_ref.dtype)


def feed_forward(rows, weight, w_gate_up, w_down):
    row_count, model_width = rows.shape
    hidden_count = w_down.shape[0]
    tile = max(t for t in range(16, 513, 16) if hidden_count % t == 0)
    step_count = hidden_count // tile
    return pl.pallas_call(
        functools.partial(ffn_kernel, step_count),
        grid=(step_count,),
        in_specs=[
            pl.BlockSpec((row_count, model_width), lambda j: (0, 0)),
            pl.BlockSpec((row_count, 1), lambda j: (0, 0)),
            pl.BlockSpec((2, tile, model_width), lambda j: (0, j, 0)),
            pl.BlockSpec((tile, model_width), lambda j: (j, 0)),
        ],
        out_specs=pl.BlockSpec((row_count, model_width), lambda j: (0, 0)),
        out_shape=jax.ShapeDtypeStruct((row_count, model_width), jnp.bfloat16),
        scratch_shapes=[pltpu.VMEM((row_count, model_width), jnp.float32)],
        compiler_params=pltpu.CompilerParams(vmem_limit_bytes=48 * 1024 * 1024),
        cost_estimate=pl.CostEstimate(
            flops=6 * row_count * model_width * hidden_count,
            bytes_accessed=6 * model_width * hidden_count,
            transcendentals=row_count * hidden_count,
        ),
    )(rows, weight, w_gate_up, w_down)


def expert_apply(slot_rows, slot_ids, own_expert, w_router, w_gate_up, w_down):
    logits = jnp.dot(slot_rows.astype(jnp.float32), w_router, precision=lax.Precision.HIGHEST)
    expert_count = w_router.shape[1]
    one_hot = (
        slot_ids[:, :, None] == jnp.arange(expert_count, dtype=jnp.int32)[None, None, :]
    ).astype(jnp.float32)
    chosen = jnp.sum(one_hot * logits[:, None, :], axis=-1)
    gate_probs = jax.nn.softmax(chosen, axis=-1)
    weight = jnp.sum(jnp.where(slot_ids == own_expert, gate_probs, 0.0), axis=-1)
    return feed_forward(slot_rows, weight[:, None], w_gate_up, w_down)


def shards(
    hidden_in,
    norm_attn,
    norm_ffn,
    w_qkv,
    w_out,
    w_router,
    w_gate_up,
    w_down,
    segment_ids,
    expert_ids,
):
    local_rows = hidden_in.shape[0]
    model_width = hidden_in.shape[1]
    tensor_count = lax.axis_size("tensor")
    tensor_place = lax.axis_index("tensor")
    seq_place = lax.axis_index("seq")
    group_rows = local_rows * tensor_count
    head_count = w_qkv.shape[2] // HD
    full_hidden = lax.all_gather(hidden_in, "tensor", axis=0, tiled=True)
    projected = jnp.einsum(
        "td,cdh->tch",
        rms_norm(full_hidden, norm_attn),
        w_qkv,
        preferred_element_type=jnp.float32,
    )
    positions = seq_place * group_rows + jnp.arange(group_rows, dtype=jnp.int32)
    query_rows = rotate(projected[:, 0].reshape(group_rows, head_count, HD), positions).astype(
        jnp.bfloat16
    )
    key_rows = rotate(projected[:, 1].reshape(group_rows, head_count, HD), positions).astype(
        jnp.bfloat16
    )
    value_rows = projected[:, 2].reshape(group_rows, head_count, HD).astype(jnp.bfloat16)
    kv_rows = jnp.concatenate([key_rows, value_rows], axis=-1)
    kv_cache = kv_rows.transpose(1, 0, 2)
    seq_count = lax.axis_size("seq")
    kv_flat = kv_cache.reshape(head_count * group_rows, 2 * HD)
    kv_packed = jnp.concatenate([kv_flat, pack_ids(segment_ids, 2 * HD)], axis=0)
    out_packed = jnp.concatenate([w_out, pack_ids(expert_ids, model_width)], axis=0)
    kv_packed, out_packed = lax.optimization_barrier((kv_packed, out_packed))
    arrivals = []
    for step in range(1, seq_count):
        pairs = [(i, i ^ step) for i in range(seq_count)]
        arrivals.append((lax.ppermute(kv_packed, "seq", pairs), seq_place ^ step))
    out_gathered = lax.all_gather(out_packed, "tensor", axis=0)
    full_ids = unpack_ids(out_gathered[:, w_out.shape[0] :], 2 * local_rows)
    w_out_full = out_gathered[:, : w_out.shape[0]].reshape(-1, model_width)
    start_state = (
        jnp.full((head_count, group_rows), low_score, jnp.float32),
        jnp.zeros((head_count, group_rows), jnp.float32),
        jnp.zeros((head_count, HD, group_rows), jnp.float32),
    )
    softmax_state = fold_keys(
        start_state,
        query_rows,
        segment_ids,
        positions,
        kv_rows,
        segment_ids,
        seq_place * group_rows,
    )
    for arrived, source in arrivals:
        softmax_state = fold_keys(
            softmax_state,
            query_rows,
            segment_ids,
            positions,
            arrived[: kv_flat.shape[0]]
            .reshape(head_count, group_rows, 2 * HD)
            .transpose(1, 0, 2),
            unpack_ids(arrived[kv_flat.shape[0] :], group_rows),
            source * group_rows,
        )
    running_max, denominator, weighted_sum = softmax_state
    attended = (
        (weighted_sum / denominator[:, None, :])
        .astype(jnp.bfloat16)
        .reshape(head_count * HD, group_rows)
    )
    attended, w_out_full = lax.optimization_barrier((attended, w_out_full))
    attention_sum = lax.dot_general(
        lax.all_gather(attended, "tensor", axis=0, tiled=True),
        w_out_full,
        (((0,), (0,)), ((), ())),
        preferred_element_type=jnp.float32,
    )
    full_residual = full_hidden.astype(jnp.float32) + attention_sum
    full_rows = rms_norm(full_residual, norm_ffn)
    residual = lax.dynamic_slice_in_dim(full_residual, tensor_place * local_rows, local_rows, 0)
    expert_count = w_router.shape[1]
    slice_count = tensor_count // expert_count
    own_expert = tensor_place // slice_count
    slot_count = local_rows // 2
    block_ids = full_ids.reshape(tensor_count, local_rows, 2)
    slot_tables = jax.vmap(lambda source_ids: slot_table(source_ids, own_expert, slot_count))(
        block_ids
    )
    slot_rows = jnp.einsum(
        "sjr,srd->sjd",
        slot_tables,
        full_rows.reshape(tensor_count, local_rows, model_width),
        preferred_element_type=jnp.float32,
    ).astype(jnp.bfloat16)
    slot_ids = jnp.einsum(
        "sjr,srk->sjk", slot_tables.astype(jnp.float32), block_ids.astype(jnp.float32)
    ).astype(jnp.int32)
    term_rows = expert_apply(
        slot_rows.reshape(-1, model_width),
        slot_ids.reshape(-1, 2),
        own_expert,
        w_router,
        w_gate_up,
        w_down,
    )
    placed = jnp.einsum(
        "sjr,sjd->srd",
        slot_tables,
        term_rows.reshape(tensor_count, slot_count, model_width),
        preferred_element_type=jnp.float32,
    ).reshape(group_rows, model_width)
    expert_sum = lax.psum_scatter(
        placed.astype(jnp.bfloat16), "tensor", scatter_dimension=0, tiled=True
    ).astype(jnp.float32)
    hidden_out = (residual + expert_sum).astype(jnp.bfloat16)
    return (hidden_out, kv_cache)


def solution(mesh):
    placed = (
        P(("seq", "tensor"), None),
        P(),
        P(),
        P(None, None, "tensor"),
        P("tensor", None),
        P(),
        P(None, "tensor", None),
        P("tensor", None),
        P("seq"),
        P(("seq", "tensor"), None),
    )
    return jax.shard_map(
        shards,
        mesh=mesh,
        in_specs=placed,
        out_specs=(P(("seq", "tensor"), None), P("tensor", "seq", None)),
        check_vma=False,
    )
```
